32 devices in a mesh: prow: 8 (over y, x, core), pcol: 4 (over z).
Axes of the slice: x: 2, y: 2, z: 4, core: 2. Of those that a mesh axis runs over, the one named last changes fastest.
Arguments:
- right_sides: float32 [24, 3, 4, 64, 512], P(None, None, None, 'prow', 'pcol'), may hold values from -6 to 6
- modulus: float32 [4, 64, 512], P(None, 'prow', 'pcol'), may hold values from 0.2 to 5
- margin_sides: int32 [8, 4, 4], P('prow', 'pcol'), may hold values 0 or 1
- coarse_vectors: float32 [64, 3, 4, 64, 512], P(None, None, None, 'prow', 'pcol'), may hold values from -0.01953125 to 0.01953125
- coarse_inverse: float32 [4, 64, 64], P('pcol'), may hold values from -3.009933 to 28.092708
Outputs:
- preconditioned: float32 [24, 3, 4, 64, 512], P(None, None, None, 'prow', 'pcol')
The draws below stay inside these ranges and needn't reach their ends.
All inputs are finite; a program needn't handle non-finite values. No bound on the sum of `margin_sides` on one device may be relied on, other than what follows from the above.
Results may differ from the reference program's by a relative error of at most 0.00005.
Values sent between devices are 32-bit elements; how exact they have to be, the bound alone decides.
A program may use at most 128 MiB of HBM per device.

```python
import math
import jax
import jax.numpy as jnp
from jax import lax

CX = 8
CY = 128
PLANES = 4
LOADS = 24
COARSE = 64
NX = 64
NY = 512
SUBROWS = 8
COLUMNS = 4


def draw_coarse_inverse(key, part):
    magnitude = 0.04 * float(3 * PLANES * NX * CY) ** 0.5
    diagonal_key, coupling_key = jax.random.split(key)
    diagonal = jax.random.uniform(diagonal_key, (COLUMNS, COARSE), jnp.float32, 1.0, 2.0)
    coupling = 0.08 * jnp.clip(jax.random.normal(coupling_key, (COLUMNS, COARSE, COARSE), jnp.float32), -3.0, 3.0)
    coupling = 0.5 * (coupling + jnp.swapaxes(coupling, 1, 2))
    identity = jnp.eye(COARSE, dtype=jnp.float32)
    return magnitude * (coupling + diagonal[:, :, None] * identity[None, :, :])


def with_ends(drawn, key, least, high):
    shape = drawn.shape
    place = [jax.random.randint(jax.random.fold_in(key, axis), (), 0, shape[axis]) for axis in range(len(shape))]
    drawn = drawn.at[tuple(place)].set(least)
    longest = shape.index(max(shape))
    place[longest] = (place[longest] + 1) % shape[longest]
    return drawn.at[tuple(place)].set(high)


def shard_levels(rng, dims, cuts, smallest, high):
    def one(axis_at, parts):
        draws = jax.random.uniform(jax.random.fold_in(jax.random.fold_in(rng, 6), axis_at), (parts,), jnp.float32, smallest / len(cuts), high / len(cuts))
        return jnp.repeat(jnp.exp(draws), dims[axis_at] // parts).reshape((-1,) + (1,) * (len(dims) - axis_at - 1))

    level = one(*cuts[0])
    for cut in cuts[1:]:
        level = level * one(*cut)
    return level


def noise(stream_key, extent, deviation, most, cuts=(), held_as=jnp.bfloat16):
    entries = deviation * jax.random.normal(stream_key, extent, jnp.float32)
    if cuts:
        entries = entries * shard_levels(stream_key, extent, cuts, -0.22, 0.18)
    return jnp.clip(entries, -most, most).astype(held_as)


def setup_inputs(seed: int = 0) -> dict:
    streams_of = jax.random.split(jax.random.key(seed), 6)
    right_sides = noise(streams_of[0], (LOADS, 3, PLANES, NX, NY), 1.0, 6.0, ((3, 8), (4, 4)), jnp.float32)
    modulus = jnp.clip(jnp.exp(math.log(5.0) - 3.218876 * jax.random.uniform(streams_of[1], (PLANES, NX, NY), jnp.float32) ** shard_levels(streams_of[1], (PLANES, NX, NY), ((1, 8), (2, 4)), -0.2, 0.2)), 0.2, 5.0)
    margin_sides = with_ends((jax.random.randint(streams_of[2], (SUBROWS, COLUMNS, 4), 0, 4) < 3).astype(jnp.int32), jax.random.fold_in(streams_of[2], 1), 0, 1)
    coarse_vectors = noise(streams_of[3], (COARSE, 3, PLANES, NX, NY), (3 * PLANES * NX * CY) ** -0.5, 0.01953125, ((3, 8), (4, 4)), jnp.float32)
    coarse_inverse = draw_coarse_inverse(jax.random.fold_in(streams_of[5], 71), 0)
    return dict(right_sides=right_sides, modulus=modulus, margin_sides=margin_sides, coarse_vectors=coarse_vectors, coarse_inverse=coarse_inverse)


RELAX_WEIGHT = 0.7
MASS_SHIFT = 0.5
DIAGONAL_SLOPE = 0.6 + 0.4 / 3.0
BOND_TOTAL = 44.0 / 3.0


def bond_sum(field_padded, modulus_padded, factor_rows, factor_columns):
    plane_count = modulus_padded.shape[0] - 2
    row_count = modulus_padded.shape[1] - 2
    column_count = modulus_padded.shape[2] - 2
    own_field = field_padded[..., 1:-1, 1:-1, 1:-1]
    own_modulus = modulus_padded[1:-1, 1:-1, 1:-1]
    accumulated = MASS_SHIFT * own_field
    for step_p in (-1, 0, 1):
        for step_x in (-1, 0, 1):
            for step_y in (-1, 0, 1):
                if step_p == 0 and step_x == 0 and step_y == 0:
                    continue
                length = step_p * step_p + step_x * step_x + step_y * step_y
                weight = 1.0 / (length * BOND_TOTAL)
                near_field = field_padded[..., 1 + step_p:1 + step_p + plane_count, 1 + step_x:1 + step_x + row_count, 1 + step_y:1 + step_y + column_count]
                near_modulus = modulus_padded[1 + step_p:1 + step_p + plane_count, 1 + step_x:1 + step_x + row_count, 1 + step_y:1 + step_y + column_count]
                factor = factor_rows[step_x + 1] * factor_columns[step_y + 1]
                difference = own_field - factor * near_field
                bond_weight = (0.5 * weight) * (own_modulus + near_modulus)
                direction = (step_p, step_x, step_y)
                projected = 0.0
                for component in range(3):
                    if direction[component] != 0:
                        projected = projected + direction[component] * difference[..., component, :, :, :]
                pieces = []
                for component in range(3):
                    piece = 0.6 * difference[..., component, :, :, :]
                    if direction[component] != 0:
                        piece = piece + (0.4 * direction[component] / length) * projected
                    pieces.append(piece)
                accumulated = accumulated + bond_weight * jnp.stack(pieces, axis=-4)
    return accumulated


def reference(right_sides, modulus, margin_sides, coarse_vectors, coarse_inverse):
    row_index = lax.broadcasted_iota(jnp.int32, (NX, NY), 0)
    column_index = lax.broadcasted_iota(jnp.int32, (NX, NY), 1)
    cell_sides = margin_sides[row_index // CX, column_index // CY].astype(jnp.float32)
    row_place = row_index % CX
    column_place = column_index % CY
    unity = jnp.ones((NX, NY), jnp.float32)
    factor_rows = jnp.stack([jnp.where(row_place == 0, cell_sides[:, :, 0], unity), unity, jnp.where(row_place == CX - 1, cell_sides[:, :, 1], unity)])
    factor_columns = jnp.stack([jnp.where(column_place == 0, cell_sides[:, :, 2], unity), unity, jnp.where(column_place == CY - 1, cell_sides[:, :, 3], unity)])
    diagonal = MASS_SHIFT + DIAGONAL_SLOPE * modulus
    modulus_padded = jnp.pad(modulus, 1)

    def smooth_one(load):
        first = RELAX_WEIGHT * load / diagonal
        first_padded = jnp.pad(first, ((0, 0), (1, 1), (1, 1), (1, 1)))
        applied = bond_sum(first_padded, modulus_padded, factor_rows, factor_columns)
        return first + RELAX_WEIGHT * (load - applied) / diagonal

    smoothed = lax.map(smooth_one, right_sides)
    vectors = coarse_vectors.reshape(COARSE, 3, PLANES, NX, COLUMNS, CY)
    loads = right_sides.reshape(LOADS, 3, PLANES, NX, COLUMNS, CY)
    restricted = jnp.einsum('vcpxjy,kcpxjy->jvk', vectors, loads, precision=lax.Precision.HIGHEST)
    solved = jnp.einsum('jvw,jwk->jvk', coarse_inverse, restricted, precision=lax.Precision.HIGHEST)
    lifted = jnp.einsum('jvk,vcpxjy->kcpxjy', solved, vectors, precision=lax.Precision.HIGHEST)
    return smoothed + lifted.reshape(LOADS, 3, PLANES, NX, NY)
```

```python
import functools

import jax
import jax.numpy as jnp
import ml_dtypes
import numpy as np
from jax import lax
from jax.experimental import pallas as pl
from jax.experimental.pallas import tpu as pltpu
from jax.sharding import PartitionSpec as P

RELAX_WEIGHT = 0.7
MASS_SHIFT = 0.5
DIAGONAL_SLOPE = 0.6 + 0.4 / 3.0
SCALE = 660.0
MESH = pl.DeviceIdType.MESH
F32, BF16 = jnp.float32, jnp.bfloat16
PLANES, ROWS, LANES = 4, 8, 128
OFFSETS = [
    (p, x, y)
    for p in (-1, 0, 1)
    for x in (-1, 0, 1)
    for y in (-1, 0, 1)
    if (p, x, y) != (0, 0, 0)
]


def scaled_bond(d):
    length = sum(v * v for v in d)
    d = np.array(d, np.float64)
    return 27.0 / length * np.eye(3) + 18.0 / length**2 * np.outer(d, d)


def cell(c, p, x):
    return (c * PLANES + p) * ROWS + x


def constants():
    main = np.zeros((3, 96, 128))
    edge = np.zeros((3, 2, 96, 128))
    for d in OFFSETS:
        w = scaled_bond(d)
        dp, dx, dy = d
        for p in range(PLANES):
            q = p + dp
            if not 0 <= q < PLANES:
                continue
            for x in range(ROWS):
                z = x + dx
                for c in range(3):
                    for e in range(3):
                        row, v = cell(c, p, x), w[c, e]
                        if z < 0:
                            column, source, there = 96 + e * PLANES + q, 0, cell(e, q, ROWS - 1)
                        elif z >= ROWS:
                            column, source, there = 112 + e * PLANES + q, 2, cell(e, q, 0)
                        else:
                            column, source, there = cell(e, q, z), 1, cell(e, q, z)
                        main[dy + 1, row, column] += v
                        if dy:
                            edge[source, 0 if dy < 0 else 1, row, there] += v
    main = main.reshape(288, 128)
    edge = edge.reshape(3, 192, 128)
    place = np.zeros((3, 3, 32, 128))
    for dx in (-1, 0, 1):
        for p in range(PLANES):
            for x in range(ROWS):
                z = x + dx
                if z < 0:
                    place[0, dx + 1, p * ROWS + x, p * ROWS + ROWS - 1] = 1
                elif z >= ROWS:
                    place[2, dx + 1, p * ROWS + x, p * ROWS] = 1
                else:
                    place[1, dx + 1, p * ROWS + x, p * ROWS + z] = 1
    place = place.reshape(3, 96, 128)

    def twice(a):
        return np.concatenate([a, a], -1).astype(ml_dtypes.bfloat16)

    return twice(main), twice(edge), twice(place)


def halves(x):
    high = x.astype(BF16)
    return high, (x - high.astype(F32)).astype(BF16)


def dot(a, b):
    return jnp.dot(a, b, preferred_element_type=F32)


def dot_t(a, b):
    return lax.dot_general(a, b, (((1,), (1,)), ((), ())), preferred_element_type=F32)


def kernel(
    n, m, loads,
    sides_ref, r_hbm, v_hbm, mod_ref, inv_ref, main_ref, edge_ref, place_ref,
    out_ref,
    r_vm, v_vm, f_vm, xs, vs, row_out, row_in, col_out, col_in, part_out, part_in,
    in_sem, row_ssem, row_rsem, col_ssem, col_rsem, part_ssem, part_rsem,
):
    a, b = lax.axis_index("prow"), lax.axis_index("pcol")
    pairs = loads // 2
    vectors = v_hbm.shape[0]

    load_r = pltpu.make_async_copy(r_hbm, r_vm, in_sem.at[3])
    load_r.start()
    load_v = [
        pltpu.make_async_copy(v_hbm.at[:, c], v_vm.at[c], in_sem.at[c])
        for c in range(3)
    ]
    for copy in load_v:
        copy.start()

    barrier = pltpu.get_barrier_semaphore()
    for t in range(1, n):
        pl.semaphore_signal(barrier, inc=1, device_id=(lax.rem(a + t, n), b), device_id_type=MESH)
    beside = [(u, t) for u in (-1, 1) for t in (-1, 0, 1)]
    count = n - 1

    def there(t, u):
        ok = jnp.logical_and(a + t >= 0, a + t < n)
        return jnp.logical_and(ok, jnp.logical_and(b + u >= 0, b + u < m))

    for u, t in beside:
        count = count + there(t, u).astype(jnp.int32)

        @pl.when(there(t, u))
        def _(u=u, t=t):
            pl.semaphore_signal(barrier, inc=1, device_id=(a + t, b + u), device_id_type=MESH)

    mod = mod_ref[...]
    q = RELAX_WEIGHT / (MASS_SHIFT + DIAGONAL_SLOPE * mod)
    mod96 = jnp.concatenate([mod] * 3, 0)
    q96 = jnp.concatenate([q] * 3, 0)

    load_r.wait()
    mod_last = mod_ref[pl.ds(ROWS - 1, PLANES, stride=ROWS), :]
    mod_first = mod_ref[pl.ds(0, PLANES, stride=ROWS), :]

    def first_step(j, carry):
        for i in range(2):
            base = pl.multiple_of((2 * j + i) * 96, 96)
            lanes = slice(i * LANES, (i + 1) * LANES)
            f = r_vm[pl.ds(base, 96), :] * q96
            f_vm[pl.ds(base, 96), :] = f
            row_out[0, 2 * j + i, 0:12, :] = f_vm[pl.ds(base + ROWS - 1, 12, stride=ROWS), :]
            row_out[1, 2 * j + i, 0:12, :] = f_vm[pl.ds(base, 12, stride=ROWS), :]
            row_out[0, 2 * j + i, 12:16, :] = mod_last
            row_out[1, 2 * j + i, 12:16, :] = mod_first
            for g, x in enumerate((f, f * mod96)):
                high, low = halves(x)
                xs[j, g, 0:96, lanes] = high
                xs[j, g, 128:224, lanes] = low
        return carry

    lax.fori_loop(0, pairs, first_step, 0)

    pl.semaphore_wait(barrier, count)

    def row_copy(s):
        t = 1 if s == 0 else -1
        return pltpu.make_async_remote_copy(
            row_out.at[s], row_in.at[s], row_ssem.at[s], row_rsem.at[s],
            device_id=(a + t, b), device_id_type=MESH,
        )

    row_goes = [a + 1 < n, a >= 1]
    row_comes = [a >= 1, a + 1 < n]
    for s in range(2):
        pl.when(row_goes[s])(lambda s=s: row_copy(s).start())

    row48 = lax.broadcasted_iota(jnp.int32, (2 * loads, 2 * LANES), 0)
    lane48 = lax.broadcasted_iota(jnp.int32, (2 * loads, 2 * LANES), 1)
    side48 = (row48 >= loads).astype(jnp.int32)
    load48 = row48 - loads * side48
    odd = jnp.bitwise_and(load48, 1)
    pick_lane = odd * LANES + (1 - side48) * (LANES - 1)
    put_lane = odd * LANES + side48 * (LANES - 1)
    pick = (lane48 == pick_lane).astype(F32)
    put = (lane48 == put_lane).astype(F32)

    def column_step(j, carry):
        hot = jnp.where(load48 // 2 == j, pick, 0.0).astype(BF16)
        new = []
        for g in range(2):
            new.append(carry[g] + dot_t(hot, xs[j, g, 0:96, :]) + dot_t(hot, xs[j, g, 128:224, :]))
        return tuple(new)

    columns = lax.fori_loop(0, pairs, column_step, (jnp.zeros((2 * loads, 96), F32),) * 2)
    col_out[...] = jnp.zeros_like(col_out)
    row8 = lax.broadcasted_iota(jnp.int32, (16, LANES), 0)
    lane8 = lax.broadcasted_iota(jnp.int32, (16, LANES), 1)
    hot8 = (lane8 == jnp.where(row8 >= 8, 0, LANES - 1)).astype(F32).astype(BF16)
    mod_high, mod_low = halves(mod)
    mod_columns = dot_t(hot8, mod_high) + dot_t(hot8, mod_low)
    for s in range(2):
        for g in range(2):
            col_out[s, g * loads : (g + 1) * loads, 0:96] = columns[g][s * loads : (s + 1) * loads]
        col_out[s, 2 * loads :, 0:32] = mod_columns[8 * s : 8 * s + 8]

    def col_copy(u, t):
        s = 0 if u == 1 else 1
        return pltpu.make_async_remote_copy(
            col_out.at[s], col_in.at[s, 1 - t], col_ssem.at[s, 1 - t], col_rsem.at[s, 1 - t],
            device_id=(a + t, b + u), device_id_type=MESH,
        )

    for u, t in beside:
        pl.when(there(t, u))(lambda u=u, t=t: col_copy(u, t).start())

    total = jnp.zeros((2 * loads, 2 * vectors), F32)
    for c in range(3):
        load_v[c].wait()

        def restrict_step(j, total, c=c):
            left, right = [], []
            for i in range(2):
                v = v_vm.at[c].reshape(vectors * 32, LANES)[pl.ds(2 * j + i, vectors, stride=32), :]
                v_high, v_low = halves(v)
                right.append(jnp.concatenate([v_high, v_low], 0))
                r = r_vm[pl.ds(c * 32 + 2 * j + i, loads, stride=96), :]
                left.append(r)
            both = jnp.concatenate(right, 1)
            vs[c * 16 + j] = both
            r_high, r_low = halves(jnp.concatenate(left, 1))
            r_both = jnp.concatenate([r_high.astype(F32), r_low.astype(F32)], 0).astype(BF16)
            return total + dot_t(r_both, both)

        total = lax.fori_loop(0, 16, restrict_step, total)
    upper = total[0:loads]
    part = upper + pltpu.roll(upper, vectors, 1) + total[loads:]
    part_out[...] = part
    part_in[a] = part

    def part_copy(t):
        return pltpu.make_async_remote_copy(
            part_out, part_in.at[a], part_ssem.at[t - 1], part_rsem.at[t - 1],
            device_id=(lax.rem(a + t, n), b), device_id_type=MESH,
        )

    def part_arrival(t):
        source = lax.rem(a + n - t, n)
        return pltpu.make_async_remote_copy(
            part_out, part_in.at[source], part_ssem.at[t - 1], part_rsem.at[t - 1],
            device_id=(lax.rem(a + t, n), b), device_id_type=MESH,
        )

    for t in range(1, n):
        part_copy(t).start()

    side = [sides_ref[0, i].astype(F32) for i in range(4)]
    for s in range(2):
        pl.when(row_comes[s])(lambda s=s: row_copy(s).wait_recv())

        @pl.when(jnp.logical_not(row_comes[s]))
        def _(s=s):
            row_in[s] = jnp.zeros(row_in.shape[1:], F32)

    for u, t in beside:
        s, o = (0 if u == -1 else 1), 1 + t
        pl.when(there(t, u))(lambda u=u, t=t: col_copy(-u, -t).wait_recv())

        @pl.when(jnp.logical_not(there(t, u)))
        def _(s=s, o=o):
            col_in[s, o] = jnp.zeros(col_in.shape[2:], F32)

    edges = jnp.zeros((192, LANES), F32)
    places = jnp.zeros((96, 16), F32)
    gap = jnp.zeros((64 - 2 * loads, LANES), F32)
    for o in range(3):
        across = side[0] if o == 0 else side[1] if o == 2 else 1.0
        pieces = []
        for g in range(2):
            for s in range(2):
                pieces.append(col_in[s, o, g * loads : (g + 1) * loads, :] * (side[2 + s] * across))
            pieces.append(gap)
        high, low = halves(jnp.concatenate(pieces, 0))
        edges = edges + dot_t(edge_ref[o], jnp.concatenate([high, low], 1))
        high, low = halves(jnp.concatenate([col_in[0, o, 2 * loads :, :], col_in[1, o, 2 * loads :, :]], 0))
        places = places + dot_t(place_ref[o], jnp.concatenate([high, low], 1))
    lane = lax.broadcasted_iota(jnp.int32, (96, LANES), 1)
    from_left = jnp.logical_or(lane < loads, jnp.logical_and(lane >= 64, lane < 64 + loads))
    edges = jnp.where(from_left, edges[0:96], edges[96:192])
    own = jnp.where(lane < loads, mod96[:, 0:1], mod96[:, LANES - 1 :])
    edges = jnp.where(lane < 2 * loads, own * edges + pltpu.roll(edges, 64, 1), 0.0)
    edge_high, edge_low = halves(edges[:, 0 : 2 * loads])

    low_row, high_row = row_in[0, 0, 12:16, :], row_in[1, 0, 12:16, :]
    lane32 = lax.broadcasted_iota(jnp.int32, (32, LANES), 1)
    mod3 = mod.reshape(PLANES, ROWS, LANES)
    shifted = {}
    for dx in (-1, 0, 1):
        if dx == 0:
            base = mod
        elif dx < 0:
            base = jnp.concatenate(
                [z for p in range(PLANES) for z in (low_row[p : p + 1], mod3[p, 0 : ROWS - 1])], 0)
        else:
            base = jnp.concatenate(
                [z for p in range(PLANES) for z in (mod3[p, 1:ROWS], high_row[p : p + 1])], 0)
        here = places[(dx + 1) * 32 : (dx + 2) * 32]
        shifted[dx, 0] = base
        shifted[dx, -1] = jnp.where(lane32 == 0, here[:, 0:1], pltpu.roll(base, 1, 1))
        shifted[dx, 1] = jnp.where(lane32 == LANES - 1, here[:, 8:9], pltpu.roll(base, LANES - 1, 1))
    none = jnp.zeros((ROWS, LANES), F32)
    bonds = {}
    for d in OFFSETS:
        near = shifted[d[1], d[2]]
        if d[0] < 0:
            near = jnp.concatenate([none, near[0:24]], 0)
        elif d[0] > 0:
            near = jnp.concatenate([near[8:32], none], 0)
        w = scaled_bond(d)
        for c in range(3):
            for e in range(c, 3):
                if w[c, e]:
                    bonds[c, e] = bonds.get((c, e), 0.0) + float(w[c, e]) * near
    mix = {}
    for c in range(3):
        for e in range(c, 3):
            if c == e:
                total_bond = (0.5 / SCALE) * bonds[c, e] + (0.5 * DIAGONAL_SLOPE) * mod
                mix[c, e] = 2.0 - q * (MASS_SHIFT + total_bond)
            else:
                mix[c, e] = mix[e, c] = (-0.5 / SCALE) * q * bonds[c, e]
    rows = [jnp.concatenate([mix[c, e] for c in range(3)], 0) for e in range(3)]
    weight96 = (0.5 / SCALE) * q96
    before = pltpu.roll(mod96, LANES - 1, 1)
    after = pltpu.roll(mod96, 1, 1)
    none4 = jnp.zeros((4, LANES), F32)

    def halo_mod(s):
        row = row_in[s, 0, 12:16, :]
        return jnp.concatenate([row, row, row, none4], 0)

    halo_mods = [halo_mod(0), halo_mod(1)]

    def stencil_step(j, carry):
        for i in range(2):
            lanes = slice(i * LANES, (i + 1) * LANES)
            for s in range(2):
                f = row_in[s, 2 * j + i] * side[s]
                for g, x in enumerate((f, f * halo_mods[s])):
                    high, low = halves(x)
                    xs[j, g, 96 + 16 * s : 112 + 16 * s, lanes] = high
                    xs[j, g, 224 + 16 * s : 240 + 16 * s, lanes] = low
        hot = jnp.where(load48 // 2 == j, put, 0.0).astype(BF16)
        ends = dot(edge_high, hot) + dot(edge_low, hot)
        of = dot(main_ref[...], xs[j, 0])
        oh = dot(main_ref[...], xs[j, 1])
        for i in range(2):
            lanes = slice(i * LANES, (i + 1) * LANES)
            base = pl.multiple_of((2 * j + i) * 96, 96)
            low = pltpu.roll(of[0:96, lanes] * before + oh[0:96, lanes], 1, 1)
            mid = of[96:192, lanes] * mod96 + oh[96:192, lanes]
            high = pltpu.roll(of[192:288, lanes] * after + oh[192:288, lanes], LANES - 1, 1)
            near = mid + jnp.where(lane == 0, 0.0, low) + jnp.where(lane == LANES - 1, 0.0, high)
            near = near + ends[:, lanes]
            f = f_vm[pl.ds(base, 96), :]
            value = weight96 * near
            for e in range(3):
                value = value + rows[e] * jnp.concatenate([f[32 * e : 32 * e + 32]] * 3, 0)
            out_ref[pl.ds(base, 96), :] = value
        return carry

    lax.fori_loop(0, pairs, stencil_step, 0)

    for t in range(1, n):
        part_arrival(t).wait_recv()
    restricted = part_in[0]
    for t in range(1, n):
        restricted = restricted + part_in[t]
    r_high, r_low = halves(restricted[:, 0:vectors])
    i_high, i_low = halves(inv_ref[...])
    solved = dot_t(r_high, i_high) + dot_t(r_low, i_high) + dot_t(r_high, i_low)
    s_high, s_low = halves(solved)
    s_high, s_low = s_high.astype(F32), s_low.astype(F32)
    left = jnp.concatenate(
        [
            jnp.concatenate([s_high, s_high], 1),
            jnp.concatenate([s_low, jnp.zeros_like(s_low)], 1),
        ],
        0,
    ).astype(BF16)

    def lift_step(j, carry):
        both = dot(left, vs[j])
        sums = both[0:loads] + both[loads:]
        for i in range(2):
            place = pl.ds(2 * j + i, loads, stride=96)
            out_ref[place, :] = out_ref[place, :] + sums[:, i * LANES : (i + 1) * LANES]
        return carry

    lax.fori_loop(0, 48, lift_step, 0)

    for s in range(2):
        pl.when(row_goes[s])(lambda s=s: row_copy(s).wait_send())
    for u, t in beside:
        pl.when(there(t, u))(lambda u=u, t=t: col_copy(u, t).wait_send())
    for t in range(1, n):
        part_copy(t).wait_send()


def per_device(n, m, right_sides, modulus, margin_sides, coarse_vectors, coarse_inverse):
    loads, vectors = right_sides.shape[0], coarse_vectors.shape[0]
    main, edge, place = constants()
    vmem = pl.BlockSpec(memory_space=pltpu.VMEM)
    anywhere = pl.BlockSpec(memory_space=pl.ANY)
    message = (2 * loads + 8, LANES)
    dma = pltpu.SemaphoreType.DMA
    out = pl.pallas_call(
        functools.partial(kernel, n, m, loads),
        out_shape=jax.ShapeDtypeStruct((loads * 96, LANES), F32),
        in_specs=[pl.BlockSpec(memory_space=pltpu.SMEM), anywhere, anywhere] + [vmem] * 5,
        out_specs=vmem,
        scratch_shapes=[
            pltpu.VMEM((loads * 96, LANES), F32),
            pltpu.VMEM((3, vectors, 32, LANES), F32),
            pltpu.VMEM((loads * 96, LANES), F32),
            pltpu.VMEM((loads // 2, 2, 256, 2 * LANES), BF16),
            pltpu.VMEM((48, 2 * vectors, 2 * LANES), BF16),
            pltpu.VMEM((2, loads, 16, LANES), F32),
            pltpu.VMEM((2, loads, 16, LANES), F32),
            pltpu.VMEM((2,) + message, F32),
            pltpu.VMEM((2, 3) + message, F32),
            pltpu.VMEM((loads, 2 * vectors), F32),
            pltpu.VMEM((n, loads, 2 * vectors), F32),
            dma((4,)),
            dma((2,)),
            dma((2,)),
            dma((2, 3)),
            dma((2, 3)),
            dma((n - 1,)),
            dma((n - 1,)),
        ],
        compiler_params=pltpu.CompilerParams(
            collective_id=0, has_side_effects=True, vmem_limit_bytes=40 * 1024 * 1024
        ),
        cost_estimate=pl.CostEstimate(flops=10**9, bytes_accessed=6 * 10**6, transcendentals=0),
        name="schwarz",
    )(
        margin_sides.reshape(1, 4),
        right_sides.reshape(loads * 96, LANES),
        coarse_vectors.reshape(vectors, 3, 32, LANES),
        modulus.reshape(32, LANES),
        coarse_inverse.reshape(vectors, vectors),
        jnp.asarray(main),
        jnp.asarray(edge),
        jnp.asarray(place),
    )
    return out.reshape(right_sides.shape)


def solution(mesh):
    in_specs = (
        P(None, None, None, "prow", "pcol"),
        P(None, "prow", "pcol"),
        P("prow", "pcol", None),
        P(None, None, None, "prow", "pcol"),
        P("pcol", None, None),
    )
    out_specs = P(None, None, None, "prow", "pcol")
    return jax.shard_map(
        functools.partial(per_device, mesh.shape["prow"], mesh.shape["pcol"]),
        mesh=mesh, in_specs=in_specs, out_specs=out_specs, check_vma=False,
    )
```

```python
import functools

import jax
import jax.numpy as jnp
import ml_dtypes
import numpy as np
from jax import lax
from jax.experimental import pallas as pl
from jax.experimental.pallas import tpu as pltpu
from jax.sharding import PartitionSpec as P

RELAX_WEIGHT = 0.7
MASS_SHIFT = 0.5
DIAGONAL_SLOPE = 0.6 + 0.4 / 3.0
SCALE = 660.0
MESH = pl.DeviceIdType.MESH
F32, BF16 = jnp.float32, jnp.bfloat16
PLANES, ROWS, LANES = 4, 8, 128
OFFSETS = [
    (p, x, y)
    for p in (-1, 0, 1)
    for x in (-1, 0, 1)
    for y in (-1, 0, 1)
    if (p, x, y) != (0, 0, 0)
]


def scaled_bond(d):
    length = sum(v * v for v in d)
    d = np.array(d, np.float64)
    return 27.0 / length * np.eye(3) + 18.0 / length**2 * np.outer(d, d)


def cell(c, p, x):
    return (c * PLANES + p) * ROWS + x


def constants():
    main = np.zeros((3, 96, 128))
    edge = np.zeros((3, 2, 96, 128))
    for d in OFFSETS:
        w = scaled_bond(d)
        dp, dx, dy = d
        for p in range(PLANES):
            q = p + dp
            if not 0 <= q < PLANES:
                continue
            for x in range(ROWS):
                z = x + dx
                for c in range(3):
                    for e in range(3):
                        row, v = cell(c, p, x), w[c, e]
                        if z < 0:
                            column, source, there = 96 + e * PLANES + q, 0, cell(e, q, ROWS - 1)
                        elif z >= ROWS:
                            column, source, there = 112 + e * PLANES + q, 2, cell(e, q, 0)
                        else:
                            column, source, there = cell(e, q, z), 1, cell(e, q, z)
                        main[dy + 1, row, column] += v
                        if dy:
                            edge[source, 0 if dy < 0 else 1, row, there] += v
    main = main.reshape(288, 128)
    edge = edge.reshape(3, 192, 128)
    place = np.zeros((3, 3, 32, 128))
    for dx in (-1, 0, 1):
        for p in range(PLANES):
            for x in range(ROWS):
                z = x + dx
                if z < 0:
                    place[0, dx + 1, p * ROWS + x, p * ROWS + ROWS - 1] = 1
                elif z >= ROWS:
                    place[2, dx + 1, p * ROWS + x, p * ROWS] = 1
                else:
                    place[1, dx + 1, p * ROWS + x, p * ROWS + z] = 1
    place = place.reshape(3, 96, 128)

    def twice(a):
        return np.concatenate([a, a], -1).astype(ml_dtypes.bfloat16)

    return twice(main), twice(edge), twice(place)


def halves(x):
    high = x.astype(BF16)
    return high, (x - high.astype(F32)).astype(BF16)


def dot(a, b):
    return jnp.dot(a, b, preferred_element_type=F32)


def dot_t(a, b):
    return lax.dot_general(a, b, (((1,), (1,)), ((), ())), preferred_element_type=F32)


def kernel(
    n, m, loads,
    sides_hbm, r_hbm, v_hbm, mod_hbm, inv_hbm, main_hbm, edge_hbm, place_hbm,
    out_ref,
    sides_ref, mod_ref, inv_ref, main_ref, edge_ref, place_ref, r_vm, v_vm, f_vm, xs, vs, row_out, row_in, col_out, col_in, part_out, part_in,
    in_sem, row_ssem, row_rsem, col_ssem, col_rsem, part_ssem, part_rsem,
):
    a, b = lax.axis_index("prow"), lax.axis_index("pcol")
    pairs = loads // 2
    vectors = v_hbm.shape[0]

    load_mod = pltpu.make_async_copy(mod_hbm, mod_ref, in_sem.at[4])
    load_mod.start()
    load_r = pltpu.make_async_copy(r_hbm, r_vm, in_sem.at[3])
    load_r.start()
    load_v = [
        pltpu.make_async_copy(v_hbm.at[:, c], v_vm.at[c], in_sem.at[c])
        for c in range(3)
    ]
    load_rest = [
        pltpu.make_async_copy(source, target, in_sem.at[5 + i])
        for i, (source, target) in enumerate((
            (sides_hbm, sides_ref), (inv_hbm, inv_ref), (main_hbm, main_ref),
            (edge_hbm, edge_ref), (place_hbm, place_ref),
        ))
    ]
    for copy in load_v + load_rest:
        copy.start()

    barrier = pltpu.get_barrier_semaphore()
    for t in range(1, n):
        pl.semaphore_signal(barrier, inc=1, device_id=(lax.rem(a + t, n), b), device_id_type=MESH)
    beside = [(u, t) for u in (-1, 1) for t in (-1, 0, 1)]
    count = n - 1

    def there(t, u):
        ok = jnp.logical_and(a + t >= 0, a + t < n)
        return jnp.logical_and(ok, jnp.logical_and(b + u >= 0, b + u < m))

    for u, t in beside:
        count = count + there(t, u).astype(jnp.int32)

        @pl.when(there(t, u))
        def _(u=u, t=t):
            pl.semaphore_signal(barrier, inc=1, device_id=(a + t, b + u), device_id_type=MESH)

    load_mod.wait()
    mod = mod_ref[...]
    q = RELAX_WEIGHT / (MASS_SHIFT + DIAGONAL_SLOPE * mod)
    mod96 = jnp.concatenate([mod] * 3, 0)
    q96 = jnp.concatenate([q] * 3, 0)

    load_r.wait()
    mod_last = mod_ref[pl.ds(ROWS - 1, PLANES, stride=ROWS), :]
    mod_first = mod_ref[pl.ds(0, PLANES, stride=ROWS), :]

    def first_step(j, carry):
        for i in range(2):
            base = pl.multiple_of((2 * j + i) * 96, 96)
            lanes = slice(i * LANES, (i + 1) * LANES)
            f = r_vm[pl.ds(base, 96), :] * q96
            f_vm[pl.ds(base, 96), :] = f
            row_out[0, 2 * j + i, 0:12, :] = f_vm[pl.ds(base + ROWS - 1, 12, stride=ROWS), :]
            row_out[1, 2 * j + i, 0:12, :] = f_vm[pl.ds(base, 12, stride=ROWS), :]
            row_out[0, 2 * j + i, 12:16, :] = mod_last
            row_out[1, 2 * j + i, 12:16, :] = mod_first
            for g, x in enumerate((f, f * mod96)):
                high, low = halves(x)
                xs[j, g, 0:96, lanes] = high
                xs[j, g, 128:224, lanes] = low
        return carry

    lax.fori_loop(0, pairs, first_step, 0, unroll=2)

    pl.semaphore_wait(barrier, count)

    def row_copy(s):
        t = 1 if s == 0 else -1
        return pltpu.make_async_remote_copy(
            row_out.at[s], row_in.at[s], row_ssem.at[s], row_rsem.at[s],
            device_id=(a + t, b), device_id_type=MESH,
        )

    row_goes = [a + 1 < n, a >= 1]
    row_comes = [a >= 1, a + 1 < n]
    for s in range(2):
        pl.when(row_goes[s])(lambda s=s: row_copy(s).start())

    row48 = lax.broadcasted_iota(jnp.int32, (2 * loads, 2 * LANES), 0)
    lane48 = lax.broadcasted_iota(jnp.int32, (2 * loads, 2 * LANES), 1)
    side48 = (row48 >= loads).astype(jnp.int32)
    load48 = row48 - loads * side48
    odd = jnp.bitwise_and(load48, 1)
    pick_lane = odd * LANES + (1 - side48) * (LANES - 1)
    put_lane = odd * LANES + side48 * (LANES - 1)
    pick = (lane48 == pick_lane).astype(F32)
    put = (lane48 == put_lane).astype(F32)

    def column_step(j, carry):
        hot = jnp.where(load48 // 2 == j, pick, 0.0).astype(BF16)
        new = []
        for g in range(2):
            new.append(carry[g] + dot_t(hot, xs[j, g, 0:96, :]) + dot_t(hot, xs[j, g, 128:224, :]))
        return tuple(new)

    columns = lax.fori_loop(0, pairs, column_step, (jnp.zeros((2 * loads, 96), F32),) * 2, unroll=4)
    col_out[...] = jnp.zeros_like(col_out)
    row8 = lax.broadcasted_iota(jnp.int32, (16, LANES), 0)
    lane8 = lax.broadcasted_iota(jnp.int32, (16, LANES), 1)
    hot8 = (lane8 == jnp.where(row8 >= 8, 0, LANES - 1)).astype(F32).astype(BF16)
    mod_high, mod_low = halves(mod)
    mod_columns = dot_t(hot8, mod_high) + dot_t(hot8, mod_low)
    for s in range(2):
        for g in range(2):
            col_out[s, g * loads : (g + 1) * loads, 0:96] = columns[g][s * loads : (s + 1) * loads]
        col_out[s, 2 * loads :, 0:32] = mod_columns[8 * s : 8 * s + 8]

    def col_copy(u, t):
        s = 0 if u == 1 else 1
        return pltpu.make_async_remote_copy(
            col_out.at[s], col_in.at[s, 1 - t], col_ssem.at[s, 1 - t], col_rsem.at[s, 1 - t],
            device_id=(a + t, b + u), device_id_type=MESH,
        )

    for u, t in beside:
        pl.when(there(t, u))(lambda u=u, t=t: col_copy(u, t).start())

    total = jnp.zeros((2 * loads, 2 * vectors), F32)
    for c in range(3):
        load_v[c].wait()

        def restrict_step(j, total, c=c):
            blocks = []
            for h in range(4):
                left, right = [], []
                for i in range(2):
                    at = 8 * j + 2 * h + i
                    v = v_vm.at[c].reshape(vectors * 32, LANES)[pl.ds(at, vectors, stride=32), :]
                    v_high, v_low = halves(v)
                    right.append(jnp.concatenate([v_high, v_low], 0))
                    left.append(r_vm[pl.ds(c * 32 + at, loads, stride=96), :])
                r_high, r_low = halves(jnp.concatenate(left, 1))
                r_both = jnp.concatenate([r_high.astype(F32), r_low.astype(F32)], 0).astype(BF16)
                blocks.append((r_both, jnp.concatenate(right, 1)))
            for h, (r_both, both) in enumerate(blocks):
                vs[c * 16 + 4 * j + h] = both
                total = total + dot_t(r_both, both)
            return total

        total = lax.fori_loop(0, 4, restrict_step, total)
    upper = total[0:loads]
    part = upper + pltpu.roll(upper, vectors, 1) + total[loads:]
    part_out[...] = part
    part_in[a] = part

    def part_copy(t):
        return pltpu.make_async_remote_copy(
            part_out, part_in.at[a], part_ssem.at[t - 1], part_rsem.at[t - 1],
            device_id=(lax.rem(a + t, n), b), device_id_type=MESH,
        )

    def part_arrival(t):
        source = lax.rem(a + n - t, n)
        return pltpu.make_async_remote_copy(
            part_out, part_in.at[source], part_ssem.at[t - 1], part_rsem.at[t - 1],
            device_id=(lax.rem(a + t, n), b), device_id_type=MESH,
        )

    for t in range(1, n):
        part_copy(t).start()

    for copy in load_rest:
        copy.wait()
    side = [sides_ref[0:1, i : i + 1].astype(F32) for i in range(4)]
    for s in range(2):
        pl.when(row_comes[s])(lambda s=s: row_copy(s).wait_recv())

        @pl.when(jnp.logical_not(row_comes[s]))
        def _(s=s):
            row_in[s] = jnp.zeros(row_in.shape[1:], F32)

    for u, t in beside:
        s, o = (0 if u == -1 else 1), 1 + t
        pl.when(there(t, u))(lambda u=u, t=t: col_copy(-u, -t).wait_recv())

        @pl.when(jnp.logical_not(there(t, u)))
        def _(s=s, o=o):
            col_in[s, o] = jnp.zeros(col_in.shape[2:], F32)

    edges = jnp.zeros((192, LANES), F32)
    places = jnp.zeros((96, 16), F32)
    gap = jnp.zeros((64 - 2 * loads, LANES), F32)
    for o in range(3):
        across = side[0] if o == 0 else side[1] if o == 2 else jnp.ones_like(side[0])
        pieces = []
        for g in range(2):
            for s in range(2):
                pieces.append(col_in[s, o, g * loads : (g + 1) * loads, :] * (side[2 + s] * across))
            pieces.append(gap)
        high, low = halves(jnp.concatenate(pieces, 0))
        edges = edges + dot_t(edge_ref[o], jnp.concatenate([high, low], 1))
        high, low = halves(jnp.concatenate([col_in[0, o, 2 * loads :, :], col_in[1, o, 2 * loads :, :]], 0))
        places = places + dot_t(place_ref[o], jnp.concatenate([high, low], 1))
    lane = lax.broadcasted_iota(jnp.int32, (96, LANES), 1)
    from_left = jnp.logical_or(lane < loads, jnp.logical_and(lane >= 64, lane < 64 + loads))
    edges = jnp.where(from_left, edges[0:96], edges[96:192])
    own = jnp.where(lane < loads, mod96[:, 0:1], mod96[:, LANES - 1 :])
    edges = jnp.where(lane < 2 * loads, own * edges + pltpu.roll(edges, 64, 1), 0.0)
    edge_high, edge_low = halves(edges[:, 0 : 2 * loads])

    low_row, high_row = row_in[0, 0, 12:16, :], row_in[1, 0, 12:16, :]
    lane32 = lax.broadcasted_iota(jnp.int32, (32, LANES), 1)
    mod3 = mod.reshape(PLANES, ROWS, LANES)
    shifted = {}
    for dx in (-1, 0, 1):
        if dx == 0:
            base = mod
        elif dx < 0:
            base = jnp.concatenate(
                [z for p in range(PLANES) for z in (low_row[p : p + 1], mod3[p, 0 : ROWS - 1])], 0)
        else:
            base = jnp.concatenate(
                [z for p in range(PLANES) for z in (mod3[p, 1:ROWS], high_row[p : p + 1])], 0)
        here = places[(dx + 1) * 32 : (dx + 2) * 32]
        shifted[dx, 0] = base
        shifted[dx, -1] = jnp.where(lane32 == 0, here[:, 0:1], pltpu.roll(base, 1, 1))
        shifted[dx, 1] = jnp.where(lane32 == LANES - 1, here[:, 8:9], pltpu.roll(base, LANES - 1, 1))
    none = jnp.zeros((ROWS, LANES), F32)
    bonds = {}
    for d in OFFSETS:
        near = shifted[d[1], d[2]]
        if d[0] < 0:
            near = jnp.concatenate([none, near[0:24]], 0)
        elif d[0] > 0:
            near = jnp.concatenate([near[8:32], none], 0)
        w = scaled_bond(d)
        for c in range(3):
            for e in range(c, 3):
                if w[c, e]:
                    bonds[c, e] = bonds.get((c, e), 0.0) + float(w[c, e]) * near
    mix = {}
    for c in range(3):
        for e in range(c, 3):
            if c == e:
                total_bond = (0.5 / SCALE) * bonds[c, e] + (0.5 * DIAGONAL_SLOPE) * mod
                mix[c, e] = 2.0 - q * (MASS_SHIFT + total_bond)
            else:
                mix[c, e] = mix[e, c] = (-0.5 / SCALE) * q * bonds[c, e]
    rows = [jnp.concatenate([mix[c, e] for c in range(3)], 0) for e in range(3)]
    weight96 = (0.5 / SCALE) * q96
    before = pltpu.roll(mod96, LANES - 1, 1)
    after = pltpu.roll(mod96, 1, 1)
    none4 = jnp.zeros((4, LANES), F32)

    def halo_mod(s):
        row = row_in[s, 0, 12:16, :]
        return jnp.concatenate([row, row, row, none4], 0)

    halo_mods = [halo_mod(0), halo_mod(1)]

    def stencil_step(j, carry):
        for i in range(2):
            lanes = slice(i * LANES, (i + 1) * LANES)
            for s in range(2):
                f = row_in[s, 2 * j + i] * side[s]
                for g, x in enumerate((f, f * halo_mods[s])):
                    high, low = halves(x)
                    xs[j, g, 96 + 16 * s : 112 + 16 * s, lanes] = high
                    xs[j, g, 224 + 16 * s : 240 + 16 * s, lanes] = low
        hot = jnp.where(load48 // 2 == j, put, 0.0).astype(BF16)
        ends = dot(edge_high, hot) + dot(edge_low, hot)
        of = dot(main_ref[...], xs[j, 0])
        oh = dot(main_ref[...], xs[j, 1])
        for i in range(2):
            lanes = slice(i * LANES, (i + 1) * LANES)
            base = pl.multiple_of((2 * j + i) * 96, 96)
            low = pltpu.roll(of[0:96, lanes] * before + oh[0:96, lanes], 1, 1)
            mid = of[96:192, lanes] * mod96 + oh[96:192, lanes]
            high = pltpu.roll(of[192:288, lanes] * after + oh[192:288, lanes], LANES - 1, 1)
            near = mid + jnp.where(lane == 0, 0.0, low) + jnp.where(lane == LANES - 1, 0.0, high)
            near = near + ends[:, lanes]
            f = f_vm[pl.ds(base, 96), :]
            value = weight96 * near
            for e in range(3):
                value = value + rows[e] * jnp.concatenate([f[32 * e : 32 * e + 32]] * 3, 0)
            out_ref[pl.ds(base, 96), :] = value
        return carry

    lax.fori_loop(0, pairs, stencil_step, 0)

    for t in range(1, n):
        part_arrival(t).wait_recv()
    restricted = part_in[0]
    for t in range(1, n):
        restricted = restricted + part_in[t]
    r_high, r_low = halves(restricted[:, 0:vectors])
    i_high, i_low = halves(inv_ref[...])
    solved = dot_t(r_high, i_high) + dot_t(r_low, i_high) + dot_t(r_high, i_low)
    s_high, s_low = halves(solved)
    s_high, s_low = s_high.astype(F32), s_low.astype(F32)
    left = jnp.concatenate(
        [
            jnp.concatenate([s_high, s_high], 1),
            jnp.concatenate([s_low, jnp.zeros_like(s_low)], 1),
        ],
        0,
    ).astype(BF16)

    def lift_step(j, carry):
        values = []
        for h in range(8):
            both = dot(left, vs[8 * j + h])
            sums = both[0:loads] + both[loads:]
            for i in range(2):
                place = pl.ds(16 * j + 2 * h + i, loads, stride=96)
                values.append((place, out_ref[place, :] + sums[:, i * LANES : (i + 1) * LANES]))
        for place, value in values:
            out_ref[place, :] = value
        return carry

    lax.fori_loop(0, 6, lift_step, 0)

    for s in range(2):
        pl.when(row_goes[s])(lambda s=s: row_copy(s).wait_send())
    for u, t in beside:
        pl.when(there(t, u))(lambda u=u, t=t: col_copy(u, t).wait_send())
    for t in range(1, n):
        part_copy(t).wait_send()


def per_device(n, m, right_sides, modulus, margin_sides, coarse_vectors, coarse_inverse):
    loads, vectors = right_sides.shape[0], coarse_vectors.shape[0]
    main, edge, place = constants()
    vmem = pl.BlockSpec(memory_space=pltpu.VMEM)
    message = (2 * loads + 8, LANES)
    dma = pltpu.SemaphoreType.DMA
    out = pl.pallas_call(
        functools.partial(kernel, n, m, loads),
        out_shape=jax.ShapeDtypeStruct((loads * 96, LANES), F32),
        in_specs=[pl.BlockSpec(memory_space=pltpu.HBM)] * 8,
        out_specs=vmem,
        scratch_shapes=[
            pltpu.VMEM((1, 4), jnp.int32),
            pltpu.VMEM((32, LANES), F32),
            pltpu.VMEM((vectors, vectors), F32),
            pltpu.VMEM(main.shape, BF16),
            pltpu.VMEM(edge.shape, BF16),
            pltpu.VMEM(place.shape, BF16),
            pltpu.VMEM((loads * 96, LANES), F32),
            pltpu.VMEM((3, vectors, 32, LANES), F32),
            pltpu.VMEM((loads * 96, LANES), F32),
            pltpu.VMEM((loads // 2, 2, 256, 2 * LANES), BF16),
            pltpu.VMEM((48, 2 * vectors, 2 * LANES), BF16),
            pltpu.VMEM((2, loads, 16, LANES), F32),
            pltpu.VMEM((2, loads, 16, LANES), F32),
            pltpu.VMEM((2,) + message, F32),
            pltpu.VMEM((2, 3) + message, F32),
            pltpu.VMEM((loads, 2 * vectors), F32),
            pltpu.VMEM((n, loads, 2 * vectors), F32),
            dma((10,)),
            dma((2,)),
            dma((2,)),
            dma((2, 3)),
            dma((2, 3)),
            dma((n - 1,)),
            dma((n - 1,)),
        ],
        compiler_params=pltpu.CompilerParams(
            collective_id=0, has_side_effects=True, vmem_limit_bytes=58 * 1024 * 1024
        ),
        cost_estimate=pl.CostEstimate(flops=10**9, bytes_accessed=6 * 10**6, transcendentals=0),
        name="schwarz",
    )(
        margin_sides.reshape(1, 4),
        right_sides.reshape(loads * 96, LANES),
        coarse_vectors.reshape(vectors, 3, 32, LANES),
        modulus.reshape(32, LANES),
        coarse_inverse.reshape(vectors, vectors),
        jnp.asarray(main),
        jnp.asarray(edge),
        jnp.asarray(place),
    )
    return out.reshape(right_sides.shape)


def solution(mesh):
    in_specs = (
        P(None, None, None, "prow", "pcol"),
        P(None, "prow", "pcol"),
        P("prow", "pcol", None),
        P(None, None, None, "prow", "pcol"),
        P("pcol", None, None),
    )
    out_specs = P(None, None, None, "prow", "pcol")
    return jax.shard_map(
        functools.partial(per_device, mesh.shape["prow"], mesh.shape["pcol"]),
        mesh=mesh, in_specs=in_specs, out_specs=out_specs, check_vma=False,
    )
```
